32 devices in a mesh: groups: 2 (over y), leaf: 8 (over z, x), sub: 2 (over core).
Axes of the slice: x: 2, y: 2, z: 4, core: 2. Of those that a mesh axis runs over, the one named last changes fastest.
Arguments:
- charges: float32 [32, 131072], P(None, ('groups', 'leaf', 'sub')), parts along dimension 1, may hold values from -6 to 6
- coords: float32 [3, 131072], P(None, ('groups', 'leaf', 'sub')), parts along dimension 1, may hold values from 0 to 1
- basis: bfloat16 [64, 131072], P(None, ('groups', 'leaf', 'sub')), parts along dimension 1, may hold values from -0.5 to 0.5
- near_offsets: int32 [27, 1024], P(None, ('groups', 'leaf', 'sub')), parts along dimension 1, may hold values from -16 to 16, as said below
- near_count: int32 [1024], P(('groups', 'leaf', 'sub')), parts along dimension 0, may hold values from 10 to 27
- transfer: float32 [7, 2, 64, 64], replicated, may hold values from -0.5 to 0.5
- coupling: float32 [8, 4, 64, 64], replicated, as said below
- far_used: int32 [4, 2040], P(None, 'groups'), parts along dimension 1, may hold values 0 or 1
Outputs:
- potentials: float32 [32, 131072], P(None, ('groups', 'leaf', 'sub')), parts along dimension 1
The draws below stay inside these ranges and needn't reach their ends.
There are 2 independent parts, one for each index of `groups`. The reference program is written for one: setup_inputs(seed, part) draws one part's arguments, and reference() takes and returns one part's arrays. A program takes and returns all parts, laid end to end along the dimension named above; an argument that names none is the same for every part. Nothing has to cross between parts.
Inputs may be any that keep to these rules, and one draw needn't show every extreme that they name: `near_offsets`: slot 0 of every leaf is 0 (the leaf itself); the other slots of a leaf hold distinct nonzero offsets; a source leaf may lie outside the leaves, and then adds nothing. The first near_count[i] slots of leaf i are used. `coupling`: coupling tables of order one after the product with a node's coefficients.
All inputs are finite; a program needn't handle non-finite values.
Results may differ from the reference program's by a relative error of at most 0.004.
Values sent between devices are 32-bit elements; how exact they have to be, the bound alone decides.
A program may use at most 64 MiB of HBM per device.

```python
import jax
import jax.numpy as jnp
from jax import lax

LEAF_SIZE = 128
BASIS_RANK = 64
COLUMNS = 32
NEAR_SLOTS = 27
DEV_LEVELS = 5
LEAVES_DEV = 32
UPPER_LEVELS = 2
TREE_LEVELS = 8
LEAVES = 512
POINTS = 65536


def draw_near_offsets(key, part):
    key = jax.random.fold_in(key, 5)
    reach = LEAVES_DEV // 2
    spots = jnp.arange(2 * reach, dtype=jnp.int32)
    candidates = jnp.where(spots < reach, spots - reach, spots - reach + 1)
    leaf_keys = jax.random.split(key, LEAVES)
    picked = jax.vmap(lambda single: jax.random.permutation(single, candidates))(leaf_keys)
    picked = picked[:, :NEAR_SLOTS - 1]
    offsets = jnp.concatenate([jnp.zeros((LEAVES, 1), jnp.int32), picked], axis=1)
    return offsets.T


def draw_coupling(key, part):
    key = jax.random.fold_in(key, 11)
    heights = jnp.arange(TREE_LEVELS, dtype=jnp.float32)
    factor = jnp.exp2(0.5 * heights) / jnp.sqrt(4.0 * BASIS_RANK)
    values = jnp.clip(jax.random.normal(key, (TREE_LEVELS, 4, BASIS_RANK, BASIS_RANK), jnp.float32), -6.0, 6.0)
    return values * factor[:, None, None, None]


def with_ends(drawn, rng, smallest, high):
    index_at = [jax.random.randint(jax.random.fold_in(rng, axis), (), 0, length) for axis, length in enumerate(drawn.shape)]
    widest = drawn.shape.index(max(drawn.shape))
    next_to = index_at[:widest] + [(index_at[widest] + 1) % drawn.shape[widest]] + index_at[widest + 1:]
    return drawn.at[tuple(index_at)].set(smallest).at[tuple(next_to)].set(high)


def level_of(own_key, shape, cuts, low, largest):
    factor_of, own = 1.0, jax.random.fold_in(own_key, 6)
    for dim, blocks in cuts:
        steps = jnp.exp(jax.random.uniform(jax.random.fold_in(own, dim), (blocks,), jnp.float32, low / len(cuts), largest / len(cuts)))
        factor_of = factor_of * jnp.repeat(steps, shape[dim] // blocks).reshape([-1 if axis == dim else 1 for axis in range(len(shape))])
    return factor_of


def noise(key, dims, scale, limit, shards=(), kind=jnp.bfloat16):
    drawn = jax.random.normal(key, dims, jnp.float32) * scale
    if len(shards) > 0:
        drawn = level_of(key, dims, shards, -0.22, 0.18) * drawn
    return jnp.clip(drawn, min=-limit, max=limit).astype(kind)


def setup_inputs(seed: int = 0, part: int = 0) -> dict:
    key_list = jax.random.split(jax.random.key(seed), 9)
    own_keys = jax.random.split(jax.random.fold_in(key_list[8], part), 9)
    return {
        "charges": noise(own_keys[0], (COLUMNS, POINTS), 1.0, 6.0, ((1, 16),), jnp.float32),
        "coords": jnp.clip(1.0 * jax.random.uniform(own_keys[1], (3, POINTS), jnp.float32) ** level_of(own_keys[1], (3, POINTS), ((1, 16),), -0.2, 0.2), 0.0, 1.0),
        "basis": noise(own_keys[2], (BASIS_RANK, POINTS), LEAF_SIZE ** -0.5, 0.5, ((1, 16),)),
        "near_offsets": draw_near_offsets(jax.random.fold_in(jax.random.fold_in(key_list[8], part), 71), part),
        "near_count": with_ends(jax.random.randint(own_keys[4], (LEAVES,), NEAR_SLOTS // 3 + 1, NEAR_SLOTS + 1), jax.random.fold_in(own_keys[4], 1), NEAR_SLOTS // 3 + 1, NEAR_SLOTS).astype(jnp.int32),
        "transfer": noise(key_list[5], (TREE_LEVELS - 1, 2, BASIS_RANK, BASIS_RANK), (2 * BASIS_RANK) ** -0.5, 0.5, (), jnp.float32),
        "coupling": draw_coupling(jax.random.fold_in(key_list[8], 71), part),
        "far_used": with_ends((jax.random.randint(own_keys[7], (4, 2 * LEAVES - 4), 0, 4) < 3).astype(jnp.int32), jax.random.fold_in(own_keys[7], 1), 0, 1),
    }


decay_rate = 1.7320508075688772 / 0.15
far_offsets = (-3, -2, 2, 3)
highest = lax.Precision.HIGHEST

def matern(targets, spots):
    gap_x = targets[0] - spots[0]
    gap_y = targets[1] - spots[1]
    gap_z = targets[2] - spots[2]
    scaled = decay_rate * jnp.sqrt(gap_x * gap_x + gap_y * gap_y + gap_z * gap_z)
    return ((1.0 + scaled) * jnp.exp(-scaled)).astype(jnp.bfloat16)

def lift(lower, transfer, height):
    return jnp.einsum('jk,njr->nkr', transfer[height, 0], lower[0::2], precision=highest) + jnp.einsum('jk,njr->nkr', transfer[height, 1], lower[1::2], precision=highest)

def couple(window, start, count, table, flags):
    total = jnp.zeros((count,) + window.shape[1:], jnp.float32)
    for which, offset in enumerate(far_offsets):
        piece = window[start + offset:start + offset + count]
        term = jnp.einsum('kj,njr->nkr', table[which], piece, precision=highest)
        total = total + flags[which][:, None, None].astype(jnp.float32) * term
    return total

def near_field(charges, coords, near_offsets, near_count):
    reach = LEAVES_DEV // 2
    sources = charges.astype(jnp.bfloat16).reshape(COLUMNS, LEAVES, LEAF_SIZE)
    sources = jnp.pad(sources, ((0, 0), (reach, reach), (0, 0)))
    places = jnp.pad(coords.reshape(3, LEAVES, LEAF_SIZE), ((0, 0), (reach, reach), (0, 0)))
    group = 16
    starts = jnp.arange(0, LEAVES, group, dtype=jnp.int32)
    slots = jnp.arange(NEAR_SLOTS, dtype=jnp.int32)

    def near_group(start):
        leaf_ids = start + jnp.arange(group, dtype=jnp.int32)
        offsets = lax.dynamic_slice_in_dim(near_offsets, start, group, 1)
        counts = lax.dynamic_slice_in_dim(near_count, start, group, 0)
        picks = (leaf_ids[None, :] + reach + offsets).T
        used = (slots[None, :] < counts[:, None]).astype(jnp.bfloat16)
        chosen = sources[:, picks] * used[None, :, :, None]
        spots = places[:, picks]
        targets = lax.dynamic_slice_in_dim(places, start + reach, group, 1)
        block = matern(targets[:, :, None, :, None], spots[:, :, :, None, :])
        return jnp.einsum('gspq,rgsq->rgp', block.astype(jnp.float32), chosen.astype(jnp.float32))
    parts = lax.map(near_group, starts)
    return parts.transpose(1, 0, 2, 3).reshape(COLUMNS, POINTS)

def far_field(charges, basis, transfer, coupling, far_used):
    summit = DEV_LEVELS + UPPER_LEVELS
    charges_low = charges.astype(jnp.bfloat16).reshape(COLUMNS, LEAVES, LEAF_SIZE).astype(jnp.float32)
    basis_leaf = basis.reshape(BASIS_RANK, LEAVES, LEAF_SIZE).astype(jnp.float32)
    levels = [jnp.einsum('kns,rns->nkr', basis_leaf, charges_low)]
    for height in range(summit):
        levels.append(lift(levels[-1], transfer, height))
    totals = None
    for height in range(summit, -1, -1):
        nodes = levels[height]
        count = nodes.shape[0]
        base = 2 * LEAVES - 2 * count
        flags = far_used[:, base:base + count]
        padded = jnp.pad(nodes, ((3, 3), (0, 0), (0, 0)))
        own = couple(padded, 3, count, coupling[height], flags)
        if totals is None:
            totals = own
        else:
            first = jnp.einsum('jk,nkr->njr', transfer[height, 0], totals, precision=highest)
            second = jnp.einsum('jk,nkr->njr', transfer[height, 1], totals, precision=highest)
            totals = own + jnp.stack([first, second], 1).reshape(own.shape)
    leaf_coef = totals.astype(jnp.bfloat16).astype(jnp.float32)
    return jnp.einsum('kns,nkr->rns', basis_leaf, leaf_coef).reshape(COLUMNS, POINTS)

def reference(charges, coords, basis, near_offsets, near_count, transfer, coupling, far_used):
    far_part = far_field(charges, basis, transfer, coupling, far_used)
    near_part = near_field(charges, coords, near_offsets, near_count)
    return far_part + near_part
```

```python
import functools

import jax
import jax.numpy as jnp
from jax import lax
from jax.experimental import pallas as pl
from jax.experimental.pallas import tpu as pltpu
from jax.sharding import PartitionSpec as P

decay_rate = 1.7320508075688772 / 0.15
far_offsets = (-3, -2, 2, 3)
highest = lax.Precision.HIGHEST


def shifted(x, axis, by):
    size = lax.axis_size(axis)
    pairs = [(i, i + by) for i in range(size) if 0 <= i + by < size]
    return lax.ppermute(x, axis, pairs)


def with_halo(x, sides, width):
    for axis, dim in sides:
        size, length = (lax.axis_size(axis), x.shape[dim])
        up = [(i, (i + 1) % size) for i in range(size - 1)]
        down = [(j, i) for i, j in up]
        last = lax.slice_in_dim(x, length - width, length, axis=dim)
        first = lax.slice_in_dim(x, 0, width, axis=dim)
        before = lax.ppermute(last, axis, up)
        after = lax.ppermute(first, axis, down)
        x = jnp.concatenate([before, x, after], axis=dim)
    return x


def swapped(value, axis, stride):
    mask = 2**stride
    pairs = [(source, source ^ mask) for source in range(lax.axis_size(axis))]
    return lax.ppermute(value, axis, pairs)


def split3(x):
    one = x.astype(jnp.bfloat16).astype(jnp.float32)
    two = (x - one).astype(jnp.bfloat16).astype(jnp.float32)
    three = (x - one - two).astype(jnp.bfloat16).astype(jnp.float32)
    return one, two, three


def features(coords):
    place = (coords - 0.5) * (decay_rate * 1.4426950408889634)
    c1, c2, c3 = split3(place)
    square = place * place
    n1, n2, n3 = split3(square[0:1] + square[1:2] + square[2:3])
    ones = jnp.ones_like(n1)
    pad = jnp.zeros((8, coords.shape[1]), jnp.float32)
    source = jnp.concatenate([c1, c1, c2, c2, c1, c3, n1, n2, n3, ones, ones, ones, pad], axis=0)
    target = jnp.concatenate(
        [-2 * c1, -2 * c2, -2 * c1, -2 * c2, -2 * c3, -2 * c1, ones, ones, ones, n1, n2, n3, pad],
        axis=0,
    )
    return source, target


def near_kernel(
    chunk,
    offsets_ref,
    count_ref,
    charges_ref,
    before_ref,
    after_ref,
    coords_ref,
    coords_before_ref,
    coords_after_ref,
    basis_ref,
    coef_ref,
    out_ref,
    src_ref,
    tgt_ref,
    chg_ref,
):
    leaves = coef_ref.shape[0]
    width = charges_ref.shape[1]
    size = width // leaves
    reach = leaves // 2
    slots = offsets_ref.shape[0]
    start = 0
    for piece, place in (
        (before_ref, coords_before_ref),
        (charges_ref, coords_ref),
        (after_ref, coords_after_ref),
    ):
        source, target = features(place[...])
        for n in range(piece.shape[1] // size):
            cut = slice(n * size, (n + 1) * size)
            chg_ref[start + n] = piece[:, cut].astype(jnp.bfloat16)
            src_ref[start + n] = source[:, cut].T.astype(jnp.bfloat16)
            if piece is charges_ref:
                tgt_ref[n] = target[:, cut].astype(jnp.bfloat16)
        start += piece.shape[1] // size
    chg_ref[start] = jnp.zeros(chg_ref.shape[1:], jnp.bfloat16)

    def leaf_step(i, _):
        count = count_ref[i]
        target = tgt_ref[i]

        def chunk_step(k, total):
            picks = []
            used = []
            for s in range(chunk):
                slot = k * chunk + s
                pick = jnp.where(
                    slot < count, i + reach + offsets_ref[jnp.minimum(slot, slots - 1), i], start
                )
                picks.append(pick)
                used.append(jnp.minimum(pick, start - 1))
            for s in range(chunk):
                dist = jnp.dot(src_ref[used[s]], target, preferred_element_type=jnp.float32)
                dist = jnp.maximum(dist, 1e-12)
                gap = dist * lax.rsqrt(dist)
                block = ((1.0 + gap * 0.6931471805599453) * jnp.exp2(-gap)).astype(jnp.bfloat16)
                total = total + jnp.dot(
                    chg_ref[picks[s]], block, preferred_element_type=jnp.float32
                )
            return total

        cut = pl.ds(pl.multiple_of(i * size, size), size)
        total = jnp.dot(
            coef_ref[i].astype(jnp.bfloat16), basis_ref[:, cut], preferred_element_type=jnp.float32
        )
        total = lax.fori_loop(0, (count + chunk - 1) // chunk, chunk_step, total)
        out_ref[:, cut] = total
        return 0

    lax.fori_loop(0, leaves, leaf_step, 0)


def near_field(charges, before, after, coords, coords_before, coords_after, near_offsets,
               near_count, basis, coef, chunk=5):
    leaves = near_count.shape[0]
    columns, width = charges.shape
    size = width // leaves
    vmem = pl.BlockSpec(memory_space=pltpu.VMEM)
    smem = pl.BlockSpec(memory_space=pltpu.SMEM)
    return pl.pallas_call(
        functools.partial(near_kernel, chunk),
        out_shape=jax.ShapeDtypeStruct((columns, width), jnp.float32),
        in_specs=[smem, smem] + [vmem] * 8,
        out_specs=vmem,
        scratch_shapes=[
            pltpu.VMEM((2 * leaves, size, 32), jnp.bfloat16),
            pltpu.VMEM((leaves, 32, size), jnp.bfloat16),
            pltpu.VMEM((2 * leaves + 1, columns, size), jnp.bfloat16),
        ],
        compiler_params=pltpu.CompilerParams(vmem_limit_bytes=40 * 2**20),
        name="near",
    )(near_offsets, near_count, charges, before, after, coords, coords_before, coords_after,
      basis, coef)


def lift(lower, transfer, height):
    return jnp.einsum(
        "jk,njr->nkr", transfer[height, 0], lower[0::2], precision=highest
    ) + jnp.einsum("jk,njr->nkr", transfer[height, 1], lower[1::2], precision=highest)


def couple(window, start, count, table, flags):
    total = jnp.zeros((count,) + window.shape[1:], jnp.float32)
    for which, offset in enumerate(far_offsets):
        piece = window[start + offset : start + offset + count]
        term = jnp.einsum("kj,njr->nkr", table[which], piece, precision=highest)
        total = total + flags[which][:, None, None].astype(jnp.float32) * term
    return total


def edge_window(block):
    lower = shifted(block[-3:], ("leaf", "sub"), 1)
    upper = shifted(block[:3], ("leaf", "sub"), -1)
    return jnp.concatenate([lower, block, upper], axis=0)


def pair_window(block):
    below = [shifted(block, ("leaf", "sub"), spacing) for spacing in (2, 1)]
    above = [shifted(block, ("leaf", "sub"), -spacing) for spacing in (1, 2)]
    return jnp.concatenate(below + [block] + above, axis=0)


def tree_window(block, spacing):
    below = [shifted(block, ("leaf", "sub"), times * spacing) for times in (3, 2, 1)]
    above = [shifted(block, ("leaf", "sub"), -times * spacing) for times in (1, 2, 3)]
    return jnp.concatenate(below + [block] + above, axis=0)


def local(charges, coords, basis, near_offsets, near_count, transfer, coupling, far_used):
    leaf_count = near_count.shape[0]
    width = charges.shape[1]
    leaf_size = width // leaf_count
    columns = charges.shape[0]
    devices = lax.axis_size(("leaf", "sub"))
    position = lax.axis_index(("leaf", "sub"))
    dev_levels = leaf_count.bit_length() - 1
    summit = coupling.shape[0] - 1
    leaves = leaf_count * devices
    reach = leaf_count // 2
    packed = jnp.concatenate([charges, coords], axis=0)
    widened = with_halo(packed, ((("leaf", "sub"), 1),), reach * leaf_size)
    edge = reach * leaf_size
    charges_low = charges.astype(jnp.bfloat16).reshape(columns, leaf_count, leaf_size)
    basis_leaf = basis.reshape(basis.shape[0], leaf_count, leaf_size)
    levels = [
        jnp.einsum("kns,rns->nkr", basis_leaf, charges_low, preferred_element_type=jnp.float32)
    ]
    for height in range(dev_levels):
        levels.append(lift(levels[-1], transfer, height))
    windows = {}
    for height in range(dev_levels - 1):
        windows[height] = (edge_window(levels[height]), 3)
    windows[dev_levels - 1] = (pair_window(levels[dev_levels - 1]), 4)
    node = levels[dev_levels]
    for step in range(summit - dev_levels + 1):
        windows[dev_levels + step] = (tree_window(node, 2**step), 3)
        if dev_levels + step < summit:
            other = swapped(node, ("leaf", "sub"), step)
            right = position // 2**step % 2 == 1
            first = jnp.where(right, other, node)
            second = jnp.where(right, node, other)
            node = lift(jnp.concatenate([first, second], axis=0), transfer, dev_levels + step)
    totals = None
    for height in range(summit, -1, -1):
        window, start = windows[height]
        count = max(1, leaf_count >> height)
        base = 2 * leaves - 2 * (leaves >> height)
        if height >= dev_levels:
            first_node = position // 2 ** (height - dev_levels)
        else:
            first_node = position * count
        flags = lax.dynamic_slice_in_dim(far_used, base + first_node, count, 1)
        own = couple(window, start, count, coupling[height], flags)
        if totals is None:
            totals = own
        elif height >= dev_levels:
            table = jnp.where(first_node % 2 == 0, transfer[height, 0], transfer[height, 1])
            totals = own + jnp.einsum("jk,nkr->njr", table, totals, precision=highest)
        else:
            first = jnp.einsum("jk,nkr->njr", transfer[height, 0], totals, precision=highest)
            second = jnp.einsum("jk,nkr->njr", transfer[height, 1], totals, precision=highest)
            totals = own + jnp.stack([first, second], 1).reshape(own.shape)
    return near_field(
        charges,
        widened[:columns, :edge],
        widened[:columns, edge + width :],
        coords,
        widened[columns:, :edge],
        widened[columns:, edge + width :],
        near_offsets,
        near_count,
        basis,
        totals.transpose(0, 2, 1),
    )


def solution(mesh):
    in_specs = (
        P(None, ("groups", "leaf", "sub")),
        P(None, ("groups", "leaf", "sub")),
        P(None, ("groups", "leaf", "sub")),
        P(None, ("groups", "leaf", "sub")),
        P(("groups", "leaf", "sub")),
        P(),
        P(),
        P(None, "groups"),
    )
    out_specs = P(None, ("groups", "leaf", "sub"))
    return jax.shard_map(local, mesh=mesh, in_specs=in_specs, out_specs=out_specs, check_vma=False)
```

```python
import functools

import jax
import jax.numpy as jnp
from jax import lax
from jax.experimental import pallas as pl
from jax.experimental.pallas import tpu as pltpu
from jax.sharding import PartitionSpec as P

decay_rate = 1.7320508075688772 / 0.15
far_offsets = (-3, -2, 2, 3)


def split3(x):
    one = x.astype(jnp.bfloat16).astype(jnp.float32)
    two = (x - one).astype(jnp.bfloat16).astype(jnp.float32)
    three = (x - one - two).astype(jnp.bfloat16).astype(jnp.float32)
    return one, two, three


def features(coords):
    place = (coords - 0.5) * (decay_rate * 1.4426950408889634)
    c1, c2, c3 = split3(place)
    square = place * place
    n1, n2, n3 = split3(square[0:1] + square[1:2] + square[2:3])
    ones = jnp.ones_like(n1)
    pad = jnp.zeros((8, coords.shape[1]), jnp.float32)
    source = jnp.concatenate([c1, c1, c2, c2, c1, c3, n1, n2, n3, ones, ones, ones, pad], axis=0)
    target = jnp.concatenate(
        [-2 * c1, -2 * c2, -2 * c1, -2 * c2, -2 * c3, -2 * c1, ones, ones, ones, n1, n2, n3, pad],
        axis=0,
    )
    return source, target


def near_kernel(
    chunk,
    offsets_ref,
    count_ref,
    charges_ref,
    before_ref,
    after_ref,
    coords_ref,
    coords_before_ref,
    coords_after_ref,
    basis_ref,
    coef_ref,
    out_ref,
    src_ref,
    tgt_ref,
    chg_ref,
):
    leaves = coef_ref.shape[0]
    width = charges_ref.shape[1]
    size = width // leaves
    reach = leaves // 2
    slots = offsets_ref.shape[0]
    start = 0
    for piece, place in (
        (before_ref, coords_before_ref),
        (charges_ref, coords_ref),
        (after_ref, coords_after_ref),
    ):
        source, target = features(place[...])
        for n in range(piece.shape[1] // size):
            cut = slice(n * size, (n + 1) * size)
            chg_ref[start + n] = piece[:, cut].astype(jnp.bfloat16)
            src_ref[start + n] = source[:, cut].T.astype(jnp.bfloat16)
            if piece is charges_ref:
                tgt_ref[n] = target[:, cut].astype(jnp.bfloat16)
        start += piece.shape[1] // size
    chg_ref[start] = jnp.zeros(chg_ref.shape[1:], jnp.bfloat16)

    def leaf_step(i, _):
        count = count_ref[i]
        target = tgt_ref[i]

        def chunk_step(k, total):
            picks = []
            used = []
            for s in range(chunk):
                slot = k * chunk + s
                pick = jnp.where(
                    slot < count, i + reach + offsets_ref[jnp.minimum(slot, slots - 1), i], start
                )
                picks.append(pick)
                used.append(jnp.minimum(pick, start - 1))
            for s in range(chunk):
                dist = jnp.dot(src_ref[used[s]], target, preferred_element_type=jnp.float32)
                dist = jnp.maximum(dist, 1e-12)
                gap = dist * lax.rsqrt(dist)
                block = ((1.0 + gap * 0.6931471805599453) * jnp.exp2(-gap)).astype(jnp.bfloat16)
                total = total + jnp.dot(
                    chg_ref[picks[s]], block, preferred_element_type=jnp.float32
                )
            return total

        cut = pl.ds(pl.multiple_of(i * size, size), size)
        total = jnp.dot(
            coef_ref[i].astype(jnp.bfloat16), basis_ref[:, cut], preferred_element_type=jnp.float32
        )
        total = lax.fori_loop(0, (count + chunk - 1) // chunk, chunk_step, total)
        out_ref[:, cut] = total
        return 0

    lax.fori_loop(0, leaves, leaf_step, 0)


def near_field(charges, before, after, coords, coords_before, coords_after, near_offsets,
               near_count, basis, coef, chunk=5):
    leaves = near_count.shape[0]
    columns, width = charges.shape
    size = width // leaves
    vmem = pl.BlockSpec(memory_space=pltpu.VMEM)
    smem = pl.BlockSpec(memory_space=pltpu.SMEM)
    return pl.pallas_call(
        functools.partial(near_kernel, chunk),
        out_shape=jax.ShapeDtypeStruct((columns, width), jnp.float32),
        in_specs=[smem, smem] + [vmem] * 8,
        out_specs=vmem,
        scratch_shapes=[
            pltpu.VMEM((2 * leaves, size, 32), jnp.bfloat16),
            pltpu.VMEM((leaves, 32, size), jnp.bfloat16),
            pltpu.VMEM((2 * leaves + 1, columns, size), jnp.bfloat16),
        ],
        compiler_params=pltpu.CompilerParams(vmem_limit_bytes=40 * 2**20),
        name="near",
    )(near_offsets, near_count, charges, before, after, coords, coords_before, coords_after,
      basis, coef)


def dot3(a, b, side):
    dims = (((1,), (side,)), ((), ()))
    mul = functools.partial(
        lax.dot_general, dimension_numbers=dims, preferred_element_type=jnp.float32
    )
    a1, b1 = a.astype(jnp.bfloat16), b.astype(jnp.bfloat16)
    a2 = (a - a1.astype(jnp.float32)).astype(jnp.bfloat16)
    b2 = (b - b1.astype(jnp.float32)).astype(jnp.bfloat16)
    return mul(a1, b1) + (mul(a1, b2) + mul(a2, b1))


def tree_kernel(
    devices,
    subs,
    far_ref,
    charges_ref,
    coords_ref,
    basis_ref,
    transfer_ref,
    coupling_ref,
    coef_ref,
    before_ref,
    after_ref,
    coords_before_ref,
    coords_after_ref,
    *scratch,
):
    leaves, columns, rank = coef_ref.shape
    width = charges_ref.shape[1]
    size = width // leaves
    edge = before_ref.shape[1]
    dev_levels = leaves.bit_length() - 1
    summit = coupling_ref.shape[0] - 1
    windows = scratch[:dev_levels]
    uppers = scratch[dev_levels : summit + 1]
    send_sem, recv_sem, root_send, root_recv = scratch[summit + 1 :]
    position = lax.axis_index("leaf") * subs + lax.axis_index("sub")

    def device(index):
        return {"leaf": lax.div(index, subs), "sub": lax.rem(index, subs)}

    barrier = pltpu.get_barrier_semaphore()

    def greet(step, _):
        pl.semaphore_signal(
            barrier,
            inc=1,
            device_id=device(lax.rem(position + step, devices)),
            device_id_type=pl.DeviceIdType.MESH,
        )
        return 0

    lax.fori_loop(1, devices, greet, 0)

    moves = []

    def move(source, target, shift):
        index = len(moves)
        copy = pltpu.make_async_remote_copy(
            src_ref=source,
            dst_ref=target,
            send_sem=send_sem.at[index],
            recv_sem=recv_sem.at[index],
            device_id=device(lax.rem(position + shift + devices, devices)),
            device_id_type=pl.DeviceIdType.MESH,
        )
        sends = jnp.logical_and(position + shift >= 0, position + shift < devices)
        takes = jnp.logical_and(position - shift >= 0, position - shift < devices)
        pl.when(sends)(copy.start)

        @pl.when(jnp.logical_not(takes))
        def _():
            target[...] = jnp.zeros(target.shape, target.dtype)

        moves.append((copy, sends, takes))
        return index

    def arrive(index):
        pl.when(moves[index][2])(moves[index][0].wait_recv)

    level = []
    for n in range(leaves):
        cut = slice(n * size, (n + 1) * size)
        level.append(
            lax.dot_general(
                charges_ref[:, cut].astype(jnp.bfloat16),
                basis_ref[:, cut],
                (((1,), (1,)), ((), ())),
                preferred_element_type=jnp.float32,
            )
        )
    for n in range(leaves):
        windows[0][3 + n] = level[n]
    pl.semaphore_wait(barrier, devices - 1)

    def lifted(pairs, height):
        count = pairs.shape[0] // 2
        pairs = pairs.reshape(count, 2, columns, rank)
        first = pairs[:, 0].reshape(count * columns, rank)
        second = pairs[:, 1].reshape(count * columns, rank)
        total = dot3(first, transfer_ref[height, 0], 0) + dot3(second, transfer_ref[height, 1], 0)
        return total.reshape(count, columns, rank)

    waits = []
    for height in range(dev_levels):
        count = leaves >> height
        window = windows[height]
        if height < dev_levels - 1:
            low = 3
            group = [
                move(window.at[pl.ds(count, 3)], window.at[pl.ds(0, 3)], 1),
                move(window.at[pl.ds(3, 3)], window.at[pl.ds(3 + count, 3)], -1),
            ]
        else:
            low = 4
            group = [
                move(window.at[pl.ds(4, 2)], window.at[pl.ds(4 - 2 * shift, 2)], shift)
                for shift in (1, 2, -1, -2)
            ]
        waits.append(group)
        above = lifted(window[low : low + count], height)
        if height + 1 < dev_levels - 1:
            windows[height + 1][3 : 3 + count // 2] = above
        elif height + 1 < dev_levels:
            windows[height + 1][4 : 4 + count // 2] = above
        else:
            uppers[0][3 + position] = above[0]

    def root_copy(step):
        return pltpu.make_async_remote_copy(
            src_ref=uppers[0].at[3 + position],
            dst_ref=uppers[0].at[3 + position],
            send_sem=root_send.at[step],
            recv_sem=root_recv.at[position],
            device_id=device(lax.rem(position + step, devices)),
            device_id_type=pl.DeviceIdType.MESH,
        )

    def root_start(step, _):
        root_copy(step).start()
        return 0

    lax.fori_loop(1, devices, root_start, 0)
    halo = [
        move(charges_ref.at[:, pl.ds(width - edge, edge)], before_ref, 1),
        move(coords_ref.at[:, pl.ds(width - edge, edge)], coords_before_ref, 1),
        move(charges_ref.at[:, pl.ds(0, edge)], after_ref, -1),
        move(coords_ref.at[:, pl.ds(0, edge)], coords_after_ref, -1),
    ]
    total_leaves = leaves * devices

    def flag(which, height, node):
        base = 2 * total_leaves - 2 * (total_leaves >> height)
        return far_ref[which, base + node].astype(jnp.float32)

    own = []
    for height in range(dev_levels):
        for index in waits[height]:
            arrive(index)
        count = leaves >> height
        start = 3 if height < dev_levels - 1 else 4
        window = windows[height]
        total = None
        for which, offset in enumerate(far_offsets):
            rows = jnp.concatenate(
                [
                    window[start + offset + n] * flag(which, height, position * count + n)
                    for n in range(count)
                ],
                axis=0,
            )
            term = dot3(rows, coupling_ref[height, which], 1)
            total = term if total is None else total + term
        own.append(total)

    def root_wait(step, _):
        source = lax.rem(position + step, devices)
        pltpu.make_async_remote_copy(
            src_ref=uppers[0].at[3 + position],
            dst_ref=uppers[0].at[3 + source],
            send_sem=root_send.at[step],
            recv_sem=root_recv.at[source],
            device_id=device(source),
            device_id_type=pl.DeviceIdType.MESH,
        ).wait_recv()
        return 0

    lax.fori_loop(1, devices, root_wait, 0)
    blank = jnp.zeros((3, columns, rank), jnp.float32)
    for step in range(summit - dev_levels + 1):
        count = devices >> step
        upper = uppers[step]
        upper[0:3] = blank
        upper[3 + count : 6 + count] = blank
        if step + dev_levels < summit:
            group = min(8, count // 2)

            def lift_group(k, _, upper=upper, above=uppers[step + 1], step=step, group=group):
                pairs = upper[pl.ds(3 + 2 * group * k, 2 * group)]
                above[pl.ds(3 + group * k, group)] = lifted(pairs, dev_levels + step)
                return 0

            lax.fori_loop(0, count // 2 // group, lift_group, 0)
    down = None
    for step in range(summit - dev_levels, -1, -1):
        height = dev_levels + step
        node = lax.div(position, 2**step)
        total = None
        for which, offset in enumerate(far_offsets):
            piece = uppers[step][node + 3 + offset] * flag(which, height, node)
            term = dot3(piece, coupling_ref[height, which], 1)
            total = term if total is None else total + term
        if down is not None:
            total = total + dot3(down, transfer_ref[height, lax.rem(node, 2)], 1)
        down = total
    for height in range(dev_levels - 1, -1, -1):
        count = leaves >> height
        first = dot3(down, transfer_ref[height, 0], 1).reshape(count // 2, 1, columns, rank)
        second = dot3(down, transfer_ref[height, 1], 1).reshape(count // 2, 1, columns, rank)
        both = jnp.concatenate([first, second], axis=1)
        down = own[height] + both.reshape(count * columns, rank)
    coef_ref[...] = down.reshape(leaves, columns, rank)

    for index in halo:
        arrive(index)
    for copy, sends, takes in moves:
        pl.when(sends)(copy.wait_send)

    def root_done(step, _):
        root_copy(step).wait_send()
        return 0

    lax.fori_loop(1, devices, root_done, 0)


def far_field(charges, coords, basis, transfer, coupling, far_used, leaves):
    devices = lax.axis_size(("leaf", "sub"))
    subs = lax.axis_size("sub")
    columns, width = charges.shape
    rank = basis.shape[0]
    edge = leaves // 2 * (width // leaves)
    dev_levels = leaves.bit_length() - 1
    summit = coupling.shape[0] - 1
    vmem = pl.BlockSpec(memory_space=pltpu.VMEM)
    smem = pl.BlockSpec(memory_space=pltpu.SMEM)
    windows = [
        pltpu.VMEM(((leaves >> height) + (6 if height < dev_levels - 1 else 8), columns, rank), jnp.float32)
        for height in range(dev_levels)
    ]
    uppers = [
        pltpu.VMEM(((devices >> step) + 6, columns, rank), jnp.float32)
        for step in range(summit - dev_levels + 1)
    ]
    moved = 2 * (dev_levels - 1) + 4 + 4
    return pl.pallas_call(
        functools.partial(tree_kernel, devices, subs),
        out_shape=(
            jax.ShapeDtypeStruct((leaves, columns, rank), jnp.float32),
            jax.ShapeDtypeStruct((columns, edge), jnp.float32),
            jax.ShapeDtypeStruct((columns, edge), jnp.float32),
            jax.ShapeDtypeStruct((coords.shape[0], edge), jnp.float32),
            jax.ShapeDtypeStruct((coords.shape[0], edge), jnp.float32),
        ),
        in_specs=[smem] + [vmem] * 5,
        out_specs=(vmem,) * 5,
        scratch_shapes=windows
        + uppers
        + [
            pltpu.SemaphoreType.DMA((moved,)),
            pltpu.SemaphoreType.DMA((moved,)),
            pltpu.SemaphoreType.DMA((devices,)),
            pltpu.SemaphoreType.DMA((devices,)),
        ],
        compiler_params=pltpu.CompilerParams(
            collective_id=0, has_side_effects=True, vmem_limit_bytes=48 * 2**20
        ),
        name="tree",
    )(far_used, charges, coords, basis, transfer, coupling)


def local(charges, coords, basis, near_offsets, near_count, transfer, coupling, far_used):
    coef, before, after, coords_before, coords_after = far_field(
        charges, coords, basis, transfer, coupling, far_used, near_count.shape[0]
    )
    return near_field(
        charges, before, after, coords, coords_before, coords_after, near_offsets, near_count, basis, coef
    )


def solution(mesh):
    in_specs = (
        P(None, ("groups", "leaf", "sub")),
        P(None, ("groups", "leaf", "sub")),
        P(None, ("groups", "leaf", "sub")),
        P(None, ("groups", "leaf", "sub")),
        P(("groups", "leaf", "sub")),
        P(),
        P(),
        P(None, "groups"),
    )
    out_specs = P(None, ("groups", "leaf", "sub"))
    return jax.shard_map(local, mesh=mesh, in_specs=in_specs, out_specs=out_specs, check_vma=False)
```

```python
import functools

import jax
import jax.numpy as jnp
from jax import lax
from jax.experimental import pallas as pl
from jax.experimental.pallas import tpu as pltpu
from jax.sharding import PartitionSpec as P

decay_rate = 1.7320508075688772 / 0.15
far_offsets = (-3, -2, 2, 3)


def split3(x):
    one = x.astype(jnp.bfloat16).astype(jnp.float32)
    two = (x - one).astype(jnp.bfloat16).astype(jnp.float32)
    three = (x - one - two).astype(jnp.bfloat16).astype(jnp.float32)
    return one, two, three


def features(coords):
    place = (coords - 0.5) * (decay_rate * 1.4426950408889634)
    c1, c2, c3 = split3(place)
    square = place * place
    n1, n2, n3 = split3(square[0:1] + square[1:2] + square[2:3])
    ones = jnp.ones_like(n1)
    pad = jnp.zeros((8, coords.shape[1]), jnp.float32)
    source = jnp.concatenate([c1, c1, c2, c2, c1, c3, n1, n2, n3, ones, ones, ones, pad], axis=0)
    target = jnp.concatenate(
        [-2 * c1, -2 * c2, -2 * c1, -2 * c2, -2 * c3, -2 * c1, ones, ones, ones, n1, n2, n3, pad],
        axis=0,
    )
    return source, target


def matern(dist):
    dist = jnp.maximum(dist, 1e-12)
    gap = dist * lax.rsqrt(dist)
    return ((1.0 + gap * 0.6931471805599453) * jnp.exp2(-gap)).astype(jnp.bfloat16)


def near_kernel(
    chunk,
    offsets_ref,
    count_ref,
    charges_ref,
    before_ref,
    after_ref,
    coords_ref,
    coords_before_ref,
    coords_after_ref,
    basis_ref,
    coef_ref,
    out_ref,
    src_ref,
    tgt_ref,
    chg_ref,
):
    leaves = coef_ref.shape[0]
    width = charges_ref.shape[1]
    size = width // leaves
    reach = leaves // 2
    slots = offsets_ref.shape[0]
    chunks = list(range(slots, 0, -chunk))[::-1]
    start = 0
    for piece, place in (
        (before_ref, coords_before_ref),
        (charges_ref, coords_ref),
        (after_ref, coords_after_ref),
    ):
        source, target = features(place[...])
        for n in range(piece.shape[1] // size):
            cut = slice(n * size, (n + 1) * size)
            chg_ref[start + n] = piece[:, cut].astype(jnp.bfloat16)
            src_ref[start + n] = source[:, cut].T.astype(jnp.bfloat16)
            if piece is charges_ref:
                tgt_ref[n] = target[:, cut].astype(jnp.bfloat16)
        start += piece.shape[1] // size
    chg_ref[start] = jnp.zeros(chg_ref.shape[1:], jnp.bfloat16)

    def leaf_step(i, _):
        count = count_ref[i]
        target = tgt_ref[i]

        def run(chunk, total):
            picks = []
            used = []
            for s in range(chunk):
                pick = jnp.where(s < count, i + reach + offsets_ref[min(s, slots - 1), i], start)
                picks.append(pick)
                used.append(jnp.minimum(pick, start - 1))
            for s in range(chunk):
                dist = jnp.dot(src_ref[used[s]], target, preferred_element_type=jnp.float32)
                total = total + jnp.dot(
                    chg_ref[picks[s]], matern(dist), preferred_element_type=jnp.float32
                )
            return total

        cut = pl.ds(pl.multiple_of(i * size, size), size)
        total = jnp.dot(
            coef_ref[i].astype(jnp.bfloat16), basis_ref[:, cut], preferred_element_type=jnp.float32
        )
        choice = jnp.maximum(count - chunks[0] + chunk - 1, 0) // chunk
        total = lax.switch(choice, [functools.partial(run, c) for c in chunks], total)
        out_ref[:, cut] = total
        return 0

    lax.fori_loop(0, leaves, leaf_step, 0)


def near_field(charges, before, after, coords, coords_before, coords_after, near_offsets,
               near_count, basis, coef, chunk=3):
    leaves = near_count.shape[0]
    columns, width = charges.shape
    size = width // leaves
    vmem = pl.BlockSpec(memory_space=pltpu.VMEM)
    smem = pl.BlockSpec(memory_space=pltpu.SMEM)
    return pl.pallas_call(
        functools.partial(near_kernel, chunk),
        out_shape=jax.ShapeDtypeStruct((columns, width), jnp.float32),
        in_specs=[smem, smem] + [vmem] * 8,
        out_specs=vmem,
        scratch_shapes=[
            pltpu.VMEM((2 * leaves, size, 32), jnp.bfloat16),
            pltpu.VMEM((leaves, 32, size), jnp.bfloat16),
            pltpu.VMEM((2 * leaves + 1, columns, size), jnp.bfloat16),
        ],
        compiler_params=pltpu.CompilerParams(vmem_limit_bytes=40 * 2**20),
        name="near",
    )(near_offsets, near_count, charges, before, after, coords, coords_before, coords_after,
      basis, coef)


def dot3(a, b, side):
    dims = (((1,), (side,)), ((), ()))
    mul = functools.partial(
        lax.dot_general, dimension_numbers=dims, preferred_element_type=jnp.float32
    )
    a1, b1 = a.astype(jnp.bfloat16), b.astype(jnp.bfloat16)
    a2 = (a - a1.astype(jnp.float32)).astype(jnp.bfloat16)
    b2 = (b - b1.astype(jnp.float32)).astype(jnp.bfloat16)
    return mul(a1, b1) + (mul(a1, b2) + mul(a2, b1))


def tree_kernel(
    devices,
    subs,
    far_ref,
    charges_ref,
    coords_ref,
    basis_ref,
    transfer_ref,
    coupling_ref,
    coef_ref,
    before_ref,
    after_ref,
    coords_before_ref,
    coords_after_ref,
    *scratch,
):
    leaves, columns, rank = coef_ref.shape
    width = charges_ref.shape[1]
    size = width // leaves
    edge = before_ref.shape[1]
    dev_levels = leaves.bit_length() - 1
    summit = coupling_ref.shape[0] - 1
    windows = scratch[:dev_levels]
    uppers = scratch[dev_levels : summit + 1]
    send_sem, recv_sem, root_send, root_recv = scratch[summit + 1 :]
    position = lax.axis_index("leaf") * subs + lax.axis_index("sub")

    def device(index):
        return {"leaf": lax.div(index, subs), "sub": lax.rem(index, subs)}

    barrier = pltpu.get_barrier_semaphore()

    def greet(step, _):
        pl.semaphore_signal(
            barrier,
            inc=1,
            device_id=device(lax.rem(position + step, devices)),
            device_id_type=pl.DeviceIdType.MESH,
        )
        return 0

    lax.fori_loop(1, devices, greet, 0)

    moves = []

    def move(source, target, shift):
        index = len(moves)
        copy = pltpu.make_async_remote_copy(
            src_ref=source,
            dst_ref=target,
            send_sem=send_sem.at[index],
            recv_sem=recv_sem.at[index],
            device_id=device(lax.rem(position + shift + devices, devices)),
            device_id_type=pl.DeviceIdType.MESH,
        )
        sends = jnp.logical_and(position + shift >= 0, position + shift < devices)
        takes = jnp.logical_and(position - shift >= 0, position - shift < devices)
        pl.when(sends)(copy.start)

        @pl.when(jnp.logical_not(takes))
        def _():
            target[...] = jnp.zeros(target.shape, target.dtype)

        moves.append((copy, sends, takes))
        return index

    def arrive(index):
        pl.when(moves[index][2])(moves[index][0].wait_recv)

    level = []
    for n in range(leaves):
        cut = slice(n * size, (n + 1) * size)
        level.append(
            lax.dot_general(
                charges_ref[:, cut].astype(jnp.bfloat16),
                basis_ref[:, cut],
                (((1,), (1,)), ((), ())),
                preferred_element_type=jnp.float32,
            )
        )
    for n in range(leaves):
        windows[0][3 + n] = level[n]
    pl.semaphore_wait(barrier, devices - 1)

    def lifted(pairs, height):
        count = pairs.shape[0] // 2
        pairs = pairs.reshape(count, 2, columns, rank)
        first = pairs[:, 0].reshape(count * columns, rank)
        second = pairs[:, 1].reshape(count * columns, rank)
        total = dot3(first, transfer_ref[height, 0], 0) + dot3(second, transfer_ref[height, 1], 0)
        return total.reshape(count, columns, rank)

    waits = []
    for height in range(dev_levels):
        count = leaves >> height
        window = windows[height]
        if height < dev_levels - 1:
            low = 3
            group = [
                move(window.at[pl.ds(count, 3)], window.at[pl.ds(0, 3)], 1),
                move(window.at[pl.ds(3, 3)], window.at[pl.ds(3 + count, 3)], -1),
            ]
        else:
            low = 4
            group = [
                move(window.at[pl.ds(4, 2)], window.at[pl.ds(4 - 2 * shift, 2)], shift)
                for shift in (1, 2, -1, -2)
            ]
        waits.append(group)
        above = lifted(window[low : low + count], height)
        if height + 1 < dev_levels - 1:
            windows[height + 1][3 : 3 + count // 2] = above
        elif height + 1 < dev_levels:
            windows[height + 1][4 : 4 + count // 2] = above
        else:
            uppers[0][3 + position] = above[0]

    def root_copy(step):
        return pltpu.make_async_remote_copy(
            src_ref=uppers[0].at[3 + position],
            dst_ref=uppers[0].at[3 + position],
            send_sem=root_send.at[step],
            recv_sem=root_recv.at[position],
            device_id=device(lax.rem(position + step, devices)),
            device_id_type=pl.DeviceIdType.MESH,
        )

    def root_start(step, _):
        root_copy(step).start()
        return 0

    lax.fori_loop(1, devices, root_start, 0)
    halo = [
        move(charges_ref.at[:, pl.ds(width - edge, edge)], before_ref, 1),
        move(coords_ref.at[:, pl.ds(width - edge, edge)], coords_before_ref, 1),
        move(charges_ref.at[:, pl.ds(0, edge)], after_ref, -1),
        move(coords_ref.at[:, pl.ds(0, edge)], coords_after_ref, -1),
    ]
    total_leaves = leaves * devices

    def flag(which, height, node):
        base = 2 * total_leaves - 2 * (total_leaves >> height)
        return far_ref[which, base + node].astype(jnp.float32)

    own = []
    for height in range(dev_levels):
        for index in waits[height]:
            arrive(index)
        count = leaves >> height
        start = 3 if height < dev_levels - 1 else 4
        window = windows[height]
        total = None
        for which, offset in enumerate(far_offsets):
            rows = jnp.concatenate(
                [
                    window[start + offset + n] * flag(which, height, position * count + n)
                    for n in range(count)
                ],
                axis=0,
            )
            term = dot3(rows, coupling_ref[height, which], 1)
            total = term if total is None else total + term
        own.append(total)

    def root_wait(step, _):
        source = lax.rem(position + step, devices)
        pltpu.make_async_remote_copy(
            src_ref=uppers[0].at[3 + position],
            dst_ref=uppers[0].at[3 + source],
            send_sem=root_send.at[step],
            recv_sem=root_recv.at[source],
            device_id=device(source),
            device_id_type=pl.DeviceIdType.MESH,
        ).wait_recv()
        return 0

    lax.fori_loop(1, devices, root_wait, 0)
    blank = jnp.zeros((3, columns, rank), jnp.float32)
    for step in range(summit - dev_levels + 1):
        count = devices >> step
        upper = uppers[step]
        upper[0:3] = blank
        upper[3 + count : 6 + count] = blank
        if step + dev_levels < summit:
            group = min(8, count // 2)

            def lift_group(k, _, upper=upper, above=uppers[step + 1], step=step, group=group):
                pairs = upper[pl.ds(3 + 2 * group * k, 2 * group)]
                above[pl.ds(3 + group * k, group)] = lifted(pairs, dev_levels + step)
                return 0

            lax.fori_loop(0, count // 2 // group, lift_group, 0)
    down = None
    for step in range(summit - dev_levels, -1, -1):
        height = dev_levels + step
        node = lax.div(position, 2**step)
        total = None
        for which, offset in enumerate(far_offsets):
            piece = uppers[step][node + 3 + offset] * flag(which, height, node)
            term = dot3(piece, coupling_ref[height, which], 1)
            total = term if total is None else total + term
        if down is not None:
            total = total + dot3(down, transfer_ref[height, lax.rem(node, 2)], 1)
        down = total
    for height in range(dev_levels - 1, -1, -1):
        count = leaves >> height
        first = dot3(down, transfer_ref[height, 0], 1).reshape(count // 2, 1, columns, rank)
        second = dot3(down, transfer_ref[height, 1], 1).reshape(count // 2, 1, columns, rank)
        both = jnp.concatenate([first, second], axis=1)
        down = own[height] + both.reshape(count * columns, rank)
    coef_ref[...] = down.reshape(leaves, columns, rank)

    for index in halo:
        arrive(index)
    for copy, sends, takes in moves:
        pl.when(sends)(copy.wait_send)

    def root_done(step, _):
        root_copy(step).wait_send()
        return 0

    lax.fori_loop(1, devices, root_done, 0)


def far_field(charges, coords, basis, transfer, coupling, far_used, leaves):
    devices = lax.axis_size(("leaf", "sub"))
    subs = lax.axis_size("sub")
    columns, width = charges.shape
    rank = basis.shape[0]
    edge = leaves // 2 * (width // leaves)
    dev_levels = leaves.bit_length() - 1
    summit = coupling.shape[0] - 1
    vmem = pl.BlockSpec(memory_space=pltpu.VMEM)
    smem = pl.BlockSpec(memory_space=pltpu.SMEM)
    windows = [
        pltpu.VMEM(((leaves >> height) + (6 if height < dev_levels - 1 else 8), columns, rank), jnp.float32)
        for height in range(dev_levels)
    ]
    uppers = [
        pltpu.VMEM(((devices >> step) + 6, columns, rank), jnp.float32)
        for step in range(summit - dev_levels + 1)
    ]
    moved = 2 * (dev_levels - 1) + 4 + 4
    return pl.pallas_call(
        functools.partial(tree_kernel, devices, subs),
        out_shape=(
            jax.ShapeDtypeStruct((leaves, columns, rank), jnp.float32),
            jax.ShapeDtypeStruct((columns, edge), jnp.float32),
            jax.ShapeDtypeStruct((columns, edge), jnp.float32),
            jax.ShapeDtypeStruct((coords.shape[0], edge), jnp.float32),
            jax.ShapeDtypeStruct((coords.shape[0], edge), jnp.float32),
        ),
        in_specs=[smem] + [vmem] * 5,
        out_specs=(vmem,) * 5,
        scratch_shapes=windows
        + uppers
        + [
            pltpu.SemaphoreType.DMA((moved,)),
            pltpu.SemaphoreType.DMA((moved,)),
            pltpu.SemaphoreType.DMA((devices,)),
            pltpu.SemaphoreType.DMA((devices,)),
        ],
        compiler_params=pltpu.CompilerParams(
            collective_id=0, has_side_effects=True, vmem_limit_bytes=48 * 2**20
        ),
        name="tree",
    )(far_used, charges, coords, basis, transfer, coupling)


def local(charges, coords, basis, near_offsets, near_count, transfer, coupling, far_used):
    coef, before, after, coords_before, coords_after = far_field(
        charges, coords, basis, transfer, coupling, far_used, near_count.shape[0]
    )
    return near_field(
        charges, before, after, coords, coords_before, coords_after, near_offsets, near_count, basis, coef
    )


def solution(mesh):
    in_specs = (
        P(None, ("groups", "leaf", "sub")),
        P(None, ("groups", "leaf", "sub")),
        P(None, ("groups", "leaf", "sub")),
        P(None, ("groups", "leaf", "sub")),
        P(("groups", "leaf", "sub")),
        P(),
        P(),
        P(None, "groups"),
    )
    out_specs = P(None, ("groups", "leaf", "sub"))
    return jax.shard_map(local, mesh=mesh, in_specs=in_specs, out_specs=out_specs, check_vma=False)
```

```python
import functools

import jax
import jax.numpy as jnp
from jax import lax
from jax.experimental import pallas as pl
from jax.experimental.pallas import tpu as pltpu
from jax.sharding import PartitionSpec as P

decay_rate = 1.7320508075688772 / 0.15
far_offsets = (-3, -2, 2, 3)


def split3(x):
    one = x.astype(jnp.bfloat16).astype(jnp.float32)
    two = (x - one).astype(jnp.bfloat16).astype(jnp.float32)
    three = (x - one - two).astype(jnp.bfloat16).astype(jnp.float32)
    return one, two, three


def features(coords):
    place = (coords - 0.5) * (decay_rate * 1.4426950408889634)
    c1, c2, c3 = split3(place)
    square = place * place
    n1, n2, n3 = split3(square[0:1] + square[1:2] + square[2:3])
    ones = jnp.ones_like(n1)
    pad = jnp.zeros((8, coords.shape[1]), jnp.float32)
    source = jnp.concatenate([c1, c1, c2, c2, c1, c3, n1, n2, n3, ones, ones, ones, pad], axis=0)
    target = jnp.concatenate(
        [-2 * c1, -2 * c2, -2 * c1, -2 * c2, -2 * c3, -2 * c1, ones, ones, ones, n1, n2, n3, pad],
        axis=0,
    )
    return source, target


def matern(dist):
    dist = jnp.maximum(dist, 1e-12)
    gap = dist * lax.rsqrt(dist)
    return ((1.0 + gap * 0.6931471805599453) * jnp.exp2(-gap)).astype(jnp.bfloat16)


def near_kernel(
    chunk,
    offsets_ref,
    count_ref,
    *refs,
):
    out_ref, src_ref, tgt_ref, chg_ref, load_sem = refs[8:13]
    held = refs[13:]
    loads = [
        pltpu.make_async_copy(source, target, load_sem.at[index])
        for index, (source, target) in enumerate(zip(refs[:8], held))
    ]
    for load in loads:
        load.start()
    for load in loads:
        load.wait()
    (
        charges_ref,
        before_ref,
        after_ref,
        coords_ref,
        coords_before_ref,
        coords_after_ref,
        basis_ref,
        coef_ref,
    ) = held
    leaves = coef_ref.shape[0]
    width = charges_ref.shape[1]
    size = width // leaves
    reach = leaves // 2
    slots = offsets_ref.shape[0]
    chunks = list(range(slots, 0, -chunk))[::-1]
    start = 0
    for piece, place in (
        (before_ref, coords_before_ref),
        (charges_ref, coords_ref),
        (after_ref, coords_after_ref),
    ):
        source, target = features(place[...])
        for n in range(piece.shape[1] // size):
            cut = slice(n * size, (n + 1) * size)
            chg_ref[start + n] = piece[:, cut].astype(jnp.bfloat16)
            src_ref[start + n] = source[:, cut].T.astype(jnp.bfloat16)
            if piece is charges_ref:
                tgt_ref[n] = target[:, cut].astype(jnp.bfloat16)
        start += piece.shape[1] // size
    chg_ref[start] = jnp.zeros(chg_ref.shape[1:], jnp.bfloat16)

    def leaf_step(i, _):
        count = count_ref[i]
        target = tgt_ref[i]

        def run(chunk, total):
            picks = []
            used = []
            for s in range(chunk):
                pick = jnp.where(s < count, i + reach + offsets_ref[min(s, slots - 1), i], start)
                picks.append(pick)
                used.append(jnp.minimum(pick, start - 1))
            for s in range(chunk):
                dist = jnp.dot(src_ref[used[s]], target, preferred_element_type=jnp.float32)
                total = total + jnp.dot(
                    chg_ref[picks[s]], matern(dist), preferred_element_type=jnp.float32
                )
            return total

        cut = pl.ds(pl.multiple_of(i * size, size), size)
        total = jnp.dot(
            coef_ref[i].astype(jnp.bfloat16), basis_ref[:, cut], preferred_element_type=jnp.float32
        )
        choice = jnp.maximum(count - chunks[0] + chunk - 1, 0) // chunk
        total = lax.switch(choice, [functools.partial(run, c) for c in chunks], total)
        out_ref[:, cut] = total
        return 0

    lax.fori_loop(0, leaves, leaf_step, 0)


def near_field(charges, before, after, coords, coords_before, coords_after, near_offsets,
               near_count, basis, coef, chunk=3):
    leaves = near_count.shape[0]
    columns, width = charges.shape
    size = width // leaves
    operands = (charges, before, after, coords, coords_before, coords_after, basis, coef)
    vmem = pl.BlockSpec(memory_space=pltpu.VMEM)
    smem = pl.BlockSpec(memory_space=pltpu.SMEM)
    return pl.pallas_call(
        functools.partial(near_kernel, chunk),
        out_shape=jax.ShapeDtypeStruct((columns, width), jnp.float32),
        in_specs=[smem, smem] + [pl.BlockSpec(memory_space=pltpu.HBM)] * 8,
        out_specs=vmem,
        scratch_shapes=[
            pltpu.VMEM((2 * leaves, size, 32), jnp.bfloat16),
            pltpu.VMEM((leaves, 32, size), jnp.bfloat16),
            pltpu.VMEM((2 * leaves + 1, columns, size), jnp.bfloat16),
            pltpu.SemaphoreType.DMA((8,)),
        ]
        + [pltpu.VMEM(x.shape, x.dtype) for x in operands],
        compiler_params=pltpu.CompilerParams(vmem_limit_bytes=62 * 2**20),
        name="near",
    )(near_offsets, near_count, *operands)


def dot3(a, b, side):
    dims = (((1,), (side,)), ((), ()))
    mul = functools.partial(
        lax.dot_general, dimension_numbers=dims, preferred_element_type=jnp.float32
    )
    a1, b1 = a.astype(jnp.bfloat16), b.astype(jnp.bfloat16)
    a2 = (a - a1.astype(jnp.float32)).astype(jnp.bfloat16)
    b2 = (b - b1.astype(jnp.float32)).astype(jnp.bfloat16)
    return mul(a1, b1) + (mul(a1, b2) + mul(a2, b1))


def tree_kernel(
    devices,
    subs,
    far_ref,
    charges_hbm,
    coords_hbm,
    basis_hbm,
    transfer_hbm,
    coupling_hbm,
    coef_ref,
    before_ref,
    after_ref,
    coords_before_ref,
    coords_after_ref,
    *scratch,
):
    leaves, columns, rank = coef_ref.shape
    width = charges_hbm.shape[1]
    size = width // leaves
    edge = before_ref.shape[1]
    dev_levels = leaves.bit_length() - 1
    summit = coupling_hbm.shape[0] - 1
    windows = scratch[:dev_levels]
    uppers = scratch[dev_levels : summit + 1]
    send_sem, recv_sem, root_send, root_recv, load_sem = scratch[summit + 1 : summit + 6]
    held = scratch[summit + 6 :]
    loads = [
        pltpu.make_async_copy(source, target, load_sem.at[index])
        for index, (source, target) in enumerate(
            zip((charges_hbm, basis_hbm, transfer_hbm, coupling_hbm, coords_hbm), held)
        )
    ]
    for load in loads:
        load.start()
    charges_ref, basis_ref, transfer_ref, coupling_ref, coords_ref = held
    position = lax.axis_index("leaf") * subs + lax.axis_index("sub")

    def device(index):
        return {"leaf": lax.div(index, subs), "sub": lax.rem(index, subs)}

    barrier = pltpu.get_barrier_semaphore()

    def greet(step, _):
        pl.semaphore_signal(
            barrier,
            inc=1,
            device_id=device(lax.rem(position + step, devices)),
            device_id_type=pl.DeviceIdType.MESH,
        )
        return 0

    lax.fori_loop(1, devices, greet, 0)

    moves = []

    def move(source, target, shift):
        index = len(moves)
        copy = pltpu.make_async_remote_copy(
            src_ref=source,
            dst_ref=target,
            send_sem=send_sem.at[index],
            recv_sem=recv_sem.at[index],
            device_id=device(lax.rem(position + shift + devices, devices)),
            device_id_type=pl.DeviceIdType.MESH,
        )
        sends = jnp.logical_and(position + shift >= 0, position + shift < devices)
        takes = jnp.logical_and(position - shift >= 0, position - shift < devices)
        pl.when(sends)(copy.start)

        @pl.when(jnp.logical_not(takes))
        def _():
            target[...] = jnp.zeros(target.shape, target.dtype)

        moves.append((copy, sends, takes))
        return index

    def arrive(index):
        pl.when(moves[index][2])(moves[index][0].wait_recv)

    for load in loads:
        load.wait()
    level = []
    for n in range(leaves):
        cut = slice(n * size, (n + 1) * size)
        level.append(
            lax.dot_general(
                charges_ref[:, cut].astype(jnp.bfloat16),
                basis_ref[:, cut],
                (((1,), (1,)), ((), ())),
                preferred_element_type=jnp.float32,
            )
        )
    for n in range(leaves):
        windows[0][3 + n] = level[n]
    pl.semaphore_wait(barrier, devices - 1)

    def lifted(pairs, height):
        count = pairs.shape[0] // 2
        pairs = pairs.reshape(count, 2, columns, rank)
        first = pairs[:, 0].reshape(count * columns, rank)
        second = pairs[:, 1].reshape(count * columns, rank)
        total = dot3(first, transfer_ref[height, 0], 0) + dot3(second, transfer_ref[height, 1], 0)
        return total.reshape(count, columns, rank)

    waits = []
    for height in range(dev_levels):
        count = leaves >> height
        window = windows[height]
        if height < dev_levels - 1:
            low = 3
            group = [
                move(window.at[pl.ds(count, 3)], window.at[pl.ds(0, 3)], 1),
                move(window.at[pl.ds(3, 3)], window.at[pl.ds(3 + count, 3)], -1),
            ]
        else:
            low = 4
            group = [
                move(window.at[pl.ds(4, 2)], window.at[pl.ds(4 - 2 * shift, 2)], shift)
                for shift in (1, 2, -1, -2)
            ]
        waits.append(group)
        above = lifted(window[low : low + count], height)
        if height + 1 < dev_levels - 1:
            windows[height + 1][3 : 3 + count // 2] = above
        elif height + 1 < dev_levels:
            windows[height + 1][4 : 4 + count // 2] = above
        else:
            uppers[0][3 + position] = above[0]

    def root_copy(step):
        return pltpu.make_async_remote_copy(
            src_ref=uppers[0].at[3 + position],
            dst_ref=uppers[0].at[3 + position],
            send_sem=root_send.at[step],
            recv_sem=root_recv.at[position],
            device_id=device(lax.rem(position + step, devices)),
            device_id_type=pl.DeviceIdType.MESH,
        )

    def root_start(step, _):
        root_copy(step).start()
        return 0

    lax.fori_loop(1, devices, root_start, 0)
    halo = [
        move(charges_ref.at[:, pl.ds(width - edge, edge)], before_ref, 1),
        move(coords_ref.at[:, pl.ds(width - edge, edge)], coords_before_ref, 1),
        move(charges_ref.at[:, pl.ds(0, edge)], after_ref, -1),
        move(coords_ref.at[:, pl.ds(0, edge)], coords_after_ref, -1),
    ]
    total_leaves = leaves * devices

    def flag(which, height, node):
        base = 2 * total_leaves - 2 * (total_leaves >> height)
        return far_ref[which, base + node].astype(jnp.float32)

    own = []
    for height in range(dev_levels):
        for index in waits[height]:
            arrive(index)
        count = leaves >> height
        start = 3 if height < dev_levels - 1 else 4
        window = windows[height]
        total = None
        for which, offset in enumerate(far_offsets):
            rows = jnp.concatenate(
                [
                    window[start + offset + n] * flag(which, height, position * count + n)
                    for n in range(count)
                ],
                axis=0,
            )
            term = dot3(rows, coupling_ref[height, which], 1)
            total = term if total is None else total + term
        own.append(total)

    def root_wait(step, _):
        source = lax.rem(position + step, devices)
        pltpu.make_async_remote_copy(
            src_ref=uppers[0].at[3 + position],
            dst_ref=uppers[0].at[3 + source],
            send_sem=root_send.at[step],
            recv_sem=root_recv.at[source],
            device_id=device(source),
            device_id_type=pl.DeviceIdType.MESH,
        ).wait_recv()
        return 0

    lax.fori_loop(1, devices, root_wait, 0)
    blank = jnp.zeros((3, columns, rank), jnp.float32)
    for step in range(summit - dev_levels + 1):
        count = devices >> step
        upper = uppers[step]
        upper[0:3] = blank
        upper[3 + count : 6 + count] = blank
        if step + dev_levels < summit:
            group = min(8, count // 2)

            def lift_group(k, _, upper=upper, above=uppers[step + 1], step=step, group=group):
                pairs = upper[pl.ds(3 + 2 * group * k, 2 * group)]
                above[pl.ds(3 + group * k, group)] = lifted(pairs, dev_levels + step)
                return 0

            lax.fori_loop(0, count // 2 // group, lift_group, 0)
    down = None
    for step in range(summit - dev_levels, -1, -1):
        height = dev_levels + step
        node = lax.div(position, 2**step)
        total = None
        for which, offset in enumerate(far_offsets):
            piece = uppers[step][node + 3 + offset] * flag(which, height, node)
            term = dot3(piece, coupling_ref[height, which], 1)
            total = term if total is None else total + term
        if down is not None:
            total = total + dot3(down, transfer_ref[height, lax.rem(node, 2)], 1)
        down = total
    for height in range(dev_levels - 1, -1, -1):
        count = leaves >> height
        first = dot3(down, transfer_ref[height, 0], 1).reshape(count // 2, 1, columns, rank)
        second = dot3(down, transfer_ref[height, 1], 1).reshape(count // 2, 1, columns, rank)
        both = jnp.concatenate([first, second], axis=1)
        down = own[height] + both.reshape(count * columns, rank)
    coef_ref[...] = down.reshape(leaves, columns, rank)

    for index in halo:
        arrive(index)
    for copy, sends, takes in moves:
        pl.when(sends)(copy.wait_send)

    def root_done(step, _):
        root_copy(step).wait_send()
        return 0

    lax.fori_loop(1, devices, root_done, 0)


def far_field(charges, coords, basis, transfer, coupling, far_used, leaves):
    devices = lax.axis_size(("leaf", "sub"))
    subs = lax.axis_size("sub")
    columns, width = charges.shape
    rank = basis.shape[0]
    edge = leaves // 2 * (width // leaves)
    dev_levels = leaves.bit_length() - 1
    summit = coupling.shape[0] - 1
    vmem = pl.BlockSpec(memory_space=pltpu.VMEM)
    smem = pl.BlockSpec(memory_space=pltpu.SMEM)
    windows = [
        pltpu.VMEM(((leaves >> height) + (6 if height < dev_levels - 1 else 8), columns, rank), jnp.float32)
        for height in range(dev_levels)
    ]
    uppers = [
        pltpu.VMEM(((devices >> step) + 6, columns, rank), jnp.float32)
        for step in range(summit - dev_levels + 1)
    ]
    moved = 2 * (dev_levels - 1) + 4 + 4
    return pl.pallas_call(
        functools.partial(tree_kernel, devices, subs),
        out_shape=(
            jax.ShapeDtypeStruct((leaves, columns, rank), jnp.float32),
            jax.ShapeDtypeStruct((columns, edge), jnp.float32),
            jax.ShapeDtypeStruct((columns, edge), jnp.float32),
            jax.ShapeDtypeStruct((coords.shape[0], edge), jnp.float32),
            jax.ShapeDtypeStruct((coords.shape[0], edge), jnp.float32),
        ),
        in_specs=[smem] + [pl.BlockSpec(memory_space=pltpu.HBM)] * 5,
        out_specs=(vmem,) * 5,
        scratch_shapes=windows
        + uppers
        + [
            pltpu.SemaphoreType.DMA((moved,)),
            pltpu.SemaphoreType.DMA((moved,)),
            pltpu.SemaphoreType.DMA((devices,)),
            pltpu.SemaphoreType.DMA((devices,)),
            pltpu.SemaphoreType.DMA((5,)),
        ]
        + [pltpu.VMEM(x.shape, x.dtype) for x in (charges, basis, transfer, coupling, coords)],
        compiler_params=pltpu.CompilerParams(
            collective_id=0, has_side_effects=True, vmem_limit_bytes=62 * 2**20
        ),
        name="tree",
    )(far_used, charges, coords, basis, transfer, coupling)


def local(charges, coords, basis, near_offsets, near_count, transfer, coupling, far_used):
    coef, before, after, coords_before, coords_after = far_field(
        charges, coords, basis, transfer, coupling, far_used, near_count.shape[0]
    )
    return near_field(
        charges, before, after, coords, coords_before, coords_after, near_offsets, near_count, basis, coef
    )


def solution(mesh):
    in_specs = (
        P(None, ("groups", "leaf", "sub")),
        P(None, ("groups", "leaf", "sub")),
        P(None, ("groups", "leaf", "sub")),
        P(None, ("groups", "leaf", "sub")),
        P(("groups", "leaf", "sub")),
        P(),
        P(),
        P(None, "groups"),
    )
    out_specs = P(None, ("groups", "leaf", "sub"))
    return jax.shard_map(local, mesh=mesh, in_specs=in_specs, out_specs=out_specs, check_vma=False)
```

```python
import functools

import jax
import jax.numpy as jnp
from jax import lax
from jax.experimental import pallas as pl
from jax.experimental.pallas import tpu as pltpu
from jax.sharding import PartitionSpec as P

decay_rate = 1.7320508075688772 / 0.15
far_offsets = (-3, -2, 2, 3)


def split3(x):
    one = x.astype(jnp.bfloat16).astype(jnp.float32)
    two = (x - one).astype(jnp.bfloat16).astype(jnp.float32)
    three = (x - one - two).astype(jnp.bfloat16).astype(jnp.float32)
    return one, two, three


def features(coords):
    place = (coords - 0.5) * (decay_rate * 1.4426950408889634)
    c1, c2, c3 = split3(place)
    square = place * place
    n1, n2, n3 = split3(square[0:1] + square[1:2] + square[2:3])
    ones = jnp.ones_like(n1)
    pad = jnp.zeros((8, coords.shape[1]), jnp.float32)
    source = jnp.concatenate([c1, c1, c2, c2, c1, c3, n1, n2, n3, ones, ones, ones, pad], axis=0)
    target = jnp.concatenate(
        [-2 * c1, -2 * c2, -2 * c1, -2 * c2, -2 * c3, -2 * c1, ones, ones, ones, n1, n2, n3, pad],
        axis=0,
    )
    return source, target


def matern(dist):
    dist = jnp.maximum(dist, 1e-12)
    gap = dist * lax.rsqrt(dist)
    return ((1.0 + gap * 0.6931471805599453) * jnp.exp2(-gap)).astype(jnp.bfloat16)


def near_kernel(
    chunk,
    offsets_ref,
    count_ref,
    *refs,
):
    out_ref, src_ref, tgt_ref, chg_ref, load_sem = refs[8:13]
    held = refs[13:]
    loads = [
        pltpu.make_async_copy(source, target, load_sem.at[index])
        for index, (source, target) in enumerate(zip(refs[:8], held))
    ]
    for load in loads:
        load.start()
    (
        charges_ref,
        before_ref,
        after_ref,
        coords_ref,
        coords_before_ref,
        coords_after_ref,
        basis_ref,
        coef_ref,
    ) = held
    leaves = coef_ref.shape[0]
    width = charges_ref.shape[1]
    size = width // leaves
    reach = leaves // 2
    slots = offsets_ref.shape[0]
    chunks = list(range(slots, 0, -chunk))[::-1]
    start = 0
    for piece, place, needed in (
        (before_ref, coords_before_ref, (4, 1)),
        (charges_ref, coords_ref, (3, 0)),
        (after_ref, coords_after_ref, (5, 2)),
    ):
        for index in needed:
            loads[index].wait()
        source, target = features(place[...])
        for n in range(piece.shape[1] // size):
            cut = slice(n * size, (n + 1) * size)
            chg_ref[start + n] = piece[:, cut].astype(jnp.bfloat16)
            src_ref[start + n] = source[:, cut].T.astype(jnp.bfloat16)
            if piece is charges_ref:
                tgt_ref[n] = target[:, cut].astype(jnp.bfloat16)
        start += piece.shape[1] // size
    loads[6].wait()
    loads[7].wait()
    chg_ref[start] = jnp.zeros(chg_ref.shape[1:], jnp.bfloat16)

    def leaf_step(i, _):
        count = count_ref[i]
        target = tgt_ref[i]

        def run(chunk, total):
            picks = []
            used = []
            for s in range(chunk):
                pick = jnp.where(s < count, i + reach + offsets_ref[min(s, slots - 1), i], start)
                picks.append(pick)
                used.append(jnp.minimum(pick, start - 1))
            for s in range(chunk):
                dist = jnp.dot(src_ref[used[s]], target, preferred_element_type=jnp.float32)
                total = total + jnp.dot(
                    chg_ref[picks[s]], matern(dist), preferred_element_type=jnp.float32
                )
            return total

        cut = pl.ds(pl.multiple_of(i * size, size), size)
        total = jnp.dot(
            coef_ref[i].astype(jnp.bfloat16), basis_ref[:, cut], preferred_element_type=jnp.float32
        )
        choice = jnp.maximum(count - chunks[0] + chunk - 1, 0) // chunk
        total = lax.switch(choice, [functools.partial(run, c) for c in chunks], total)
        out_ref[:, cut] = total
        return 0

    lax.fori_loop(0, leaves, leaf_step, 0)


def near_field(charges, before, after, coords, coords_before, coords_after, near_offsets,
               near_count, basis, coef, chunk=3):
    leaves = near_count.shape[0]
    columns, width = charges.shape
    size = width // leaves
    operands = (charges, before, after, coords, coords_before, coords_after, basis, coef)
    vmem = pl.BlockSpec(memory_space=pltpu.VMEM)
    smem = pl.BlockSpec(memory_space=pltpu.SMEM)
    return pl.pallas_call(
        functools.partial(near_kernel, chunk),
        out_shape=jax.ShapeDtypeStruct((columns, width), jnp.float32),
        in_specs=[smem, smem] + [pl.BlockSpec(memory_space=pltpu.HBM)] * 8,
        out_specs=vmem,
        scratch_shapes=[
            pltpu.VMEM((2 * leaves, size, 32), jnp.bfloat16),
            pltpu.VMEM((leaves, 32, size), jnp.bfloat16),
            pltpu.VMEM((2 * leaves + 1, columns, size), jnp.bfloat16),
            pltpu.SemaphoreType.DMA((8,)),
        ]
        + [pltpu.VMEM(x.shape, x.dtype) for x in operands],
        compiler_params=pltpu.CompilerParams(vmem_limit_bytes=62 * 2**20),
        name="near",
    )(near_offsets, near_count, *operands)


def dot3(a, b, side):
    dims = (((1,), (side,)), ((), ()))
    mul = functools.partial(
        lax.dot_general, dimension_numbers=dims, preferred_element_type=jnp.float32
    )
    a1, b1 = a.astype(jnp.bfloat16), b.astype(jnp.bfloat16)
    a2 = (a - a1.astype(jnp.float32)).astype(jnp.bfloat16)
    b2 = (b - b1.astype(jnp.float32)).astype(jnp.bfloat16)
    return mul(a1, b1) + (mul(a1, b2) + mul(a2, b1))


def tree_kernel(
    devices,
    subs,
    far_ref,
    charges_hbm,
    coords_hbm,
    basis_hbm,
    transfer_hbm,
    coupling_hbm,
    coef_ref,
    before_ref,
    after_ref,
    coords_before_ref,
    coords_after_ref,
    *scratch,
):
    leaves, columns, rank = coef_ref.shape
    width = charges_hbm.shape[1]
    size = width // leaves
    edge = before_ref.shape[1]
    dev_levels = leaves.bit_length() - 1
    summit = coupling_hbm.shape[0] - 1
    windows = scratch[:dev_levels]
    uppers = scratch[dev_levels : summit + 1]
    send_sem, recv_sem, root_send, root_recv, load_sem = scratch[summit + 1 : summit + 6]
    held = scratch[summit + 6 :]
    loads = [
        pltpu.make_async_copy(source, target, load_sem.at[index])
        for index, (source, target) in enumerate(
            zip((charges_hbm, basis_hbm, transfer_hbm, coupling_hbm, coords_hbm), held)
        )
    ]
    for load in loads:
        load.start()
    charges_ref, basis_ref, transfer_ref, coupling_ref, coords_ref = held
    position = lax.axis_index("leaf") * subs + lax.axis_index("sub")

    def device(index):
        return {"leaf": lax.div(index, subs), "sub": lax.rem(index, subs)}

    barrier = pltpu.get_barrier_semaphore()

    def greet(step, _):
        pl.semaphore_signal(
            barrier,
            inc=1,
            device_id=device(lax.rem(position + step, devices)),
            device_id_type=pl.DeviceIdType.MESH,
        )
        return 0

    lax.fori_loop(1, devices, greet, 0)

    moves = []

    def move(source, target, shift):
        index = len(moves)
        copy = pltpu.make_async_remote_copy(
            src_ref=source,
            dst_ref=target,
            send_sem=send_sem.at[index],
            recv_sem=recv_sem.at[index],
            device_id=device(lax.rem(position + shift + devices, devices)),
            device_id_type=pl.DeviceIdType.MESH,
        )
        sends = jnp.logical_and(position + shift >= 0, position + shift < devices)
        takes = jnp.logical_and(position - shift >= 0, position - shift < devices)
        pl.when(sends)(copy.start)

        @pl.when(jnp.logical_not(takes))
        def _():
            target[...] = jnp.zeros(target.shape, target.dtype)

        moves.append((copy, sends, takes))
        return index

    def arrive(index):
        pl.when(moves[index][2])(moves[index][0].wait_recv)

    for load in loads:
        load.wait()
    level = []
    for n in range(leaves):
        cut = slice(n * size, (n + 1) * size)
        level.append(
            lax.dot_general(
                charges_ref[:, cut].astype(jnp.bfloat16),
                basis_ref[:, cut],
                (((1,), (1,)), ((), ())),
                preferred_element_type=jnp.float32,
            )
        )
    for n in range(leaves):
        windows[0][3 + n] = level[n]
    pl.semaphore_wait(barrier, devices - 1)

    def lifted(pairs, height):
        count = pairs.shape[0] // 2
        pairs = pairs.reshape(count, 2, columns, rank)
        first = pairs[:, 0].reshape(count * columns, rank)
        second = pairs[:, 1].reshape(count * columns, rank)
        total = dot3(first, transfer_ref[height, 0], 0) + dot3(second, transfer_ref[height, 1], 0)
        return total.reshape(count, columns, rank)

    waits = []
    for height in range(dev_levels):
        count = leaves >> height
        window = windows[height]
        if height < dev_levels - 1:
            low = 3
            group = [
                move(window.at[pl.ds(count, 3)], window.at[pl.ds(0, 3)], 1),
                move(window.at[pl.ds(3, 3)], window.at[pl.ds(3 + count, 3)], -1),
            ]
        else:
            low = 4
            group = [
                move(window.at[pl.ds(4, 2)], window.at[pl.ds(4 - 2 * shift, 2)], shift)
                for shift in (1, 2, -1, -2)
            ]
        waits.append(group)
        above = lifted(window[low : low + count], height)
        if height + 1 < dev_levels - 1:
            windows[height + 1][3 : 3 + count // 2] = above
        elif height + 1 < dev_levels:
            windows[height + 1][4 : 4 + count // 2] = above
        else:
            uppers[0][3 + position] = above[0]

    def root_copy(step):
        return pltpu.make_async_remote_copy(
            src_ref=uppers[0].at[3 + position],
            dst_ref=uppers[0].at[3 + position],
            send_sem=root_send.at[step],
            recv_sem=root_recv.at[position],
            device_id=device(lax.rem(position + step, devices)),
            device_id_type=pl.DeviceIdType.MESH,
        )

    def root_start(step, _):
        root_copy(step).start()
        return 0

    lax.fori_loop(1, devices, root_start, 0)
    halo = [
        move(charges_ref.at[:, pl.ds(width - edge, edge)], before_ref, 1),
        move(coords_ref.at[:, pl.ds(width - edge, edge)], coords_before_ref, 1),
        move(charges_ref.at[:, pl.ds(0, edge)], after_ref, -1),
        move(coords_ref.at[:, pl.ds(0, edge)], coords_after_ref, -1),
    ]
    total_leaves = leaves * devices

    def flag(which, height, node):
        base = 2 * total_leaves - 2 * (total_leaves >> height)
        return far_ref[which, base + node].astype(jnp.float32)

    own = []
    for height in range(dev_levels):
        for index in waits[height]:
            arrive(index)
        count = leaves >> height
        start = 3 if height < dev_levels - 1 else 4
        window = windows[height]
        total = None
        for which, offset in enumerate(far_offsets):
            rows = jnp.concatenate(
                [
                    window[start + offset + n] * flag(which, height, position * count + n)
                    for n in range(count)
                ],
                axis=0,
            )
            term = dot3(rows, coupling_ref[height, which], 1)
            total = term if total is None else total + term
        own.append(total)

    def root_wait(step, _):
        source = lax.rem(position + step, devices)
        pltpu.make_async_remote_copy(
            src_ref=uppers[0].at[3 + position],
            dst_ref=uppers[0].at[3 + source],
            send_sem=root_send.at[step],
            recv_sem=root_recv.at[source],
            device_id=device(source),
            device_id_type=pl.DeviceIdType.MESH,
        ).wait_recv()
        return 0

    lax.fori_loop(1, devices, root_wait, 0)
    blank = jnp.zeros((3, columns, rank), jnp.float32)
    for step in range(summit - dev_levels + 1):
        count = devices >> step
        upper = uppers[step]
        upper[0:3] = blank
        upper[3 + count : 6 + count] = blank
        if step + dev_levels < summit:
            group = min(8, count // 2)

            def lift_group(k, _, upper=upper, above=uppers[step + 1], step=step, group=group):
                pairs = upper[pl.ds(3 + 2 * group * k, 2 * group)]
                above[pl.ds(3 + group * k, group)] = lifted(pairs, dev_levels + step)
                return 0

            lax.fori_loop(0, count // 2 // group, lift_group, 0)
    down = None
    for step in range(summit - dev_levels, -1, -1):
        height = dev_levels + step
        node = lax.div(position, 2**step)
        total = None
        for which, offset in enumerate(far_offsets):
            piece = uppers[step][node + 3 + offset] * flag(which, height, node)
            term = dot3(piece, coupling_ref[height, which], 1)
            total = term if total is None else total + term
        if down is not None:
            total = total + dot3(down, transfer_ref[height, lax.rem(node, 2)], 1)
        down = total
    for height in range(dev_levels - 1, -1, -1):
        count = leaves >> height
        first = dot3(down, transfer_ref[height, 0], 1).reshape(count // 2, 1, columns, rank)
        second = dot3(down, transfer_ref[height, 1], 1).reshape(count // 2, 1, columns, rank)
        both = jnp.concatenate([first, second], axis=1)
        down = own[height] + both.reshape(count * columns, rank)
    coef_ref[...] = down.reshape(leaves, columns, rank)

    for index in halo:
        arrive(index)
    for copy, sends, takes in moves:
        pl.when(sends)(copy.wait_send)

    def root_done(step, _):
        root_copy(step).wait_send()
        return 0

    lax.fori_loop(1, devices, root_done, 0)


def far_field(charges, coords, basis, transfer, coupling, far_used, leaves):
    devices = lax.axis_size(("leaf", "sub"))
    subs = lax.axis_size("sub")
    columns, width = charges.shape
    rank = basis.shape[0]
    edge = leaves // 2 * (width // leaves)
    dev_levels = leaves.bit_length() - 1
    summit = coupling.shape[0] - 1
    vmem = pl.BlockSpec(memory_space=pltpu.VMEM)
    smem = pl.BlockSpec(memory_space=pltpu.SMEM)
    windows = [
        pltpu.VMEM(((leaves >> height) + (6 if height < dev_levels - 1 else 8), columns, rank), jnp.float32)
        for height in range(dev_levels)
    ]
    uppers = [
        pltpu.VMEM(((devices >> step) + 6, columns, rank), jnp.float32)
        for step in range(summit - dev_levels + 1)
    ]
    moved = 2 * (dev_levels - 1) + 4 + 4
    return pl.pallas_call(
        functools.partial(tree_kernel, devices, subs),
        out_shape=(
            jax.ShapeDtypeStruct((leaves, columns, rank), jnp.float32),
            jax.ShapeDtypeStruct((columns, edge), jnp.float32),
            jax.ShapeDtypeStruct((columns, edge), jnp.float32),
            jax.ShapeDtypeStruct((coords.shape[0], edge), jnp.float32),
            jax.ShapeDtypeStruct((coords.shape[0], edge), jnp.float32),
        ),
        in_specs=[smem] + [pl.BlockSpec(memory_space=pltpu.HBM)] * 5,
        out_specs=(vmem,) * 5,
        scratch_shapes=windows
        + uppers
        + [
            pltpu.SemaphoreType.DMA((moved,)),
            pltpu.SemaphoreType.DMA((moved,)),
            pltpu.SemaphoreType.DMA((devices,)),
            pltpu.SemaphoreType.DMA((devices,)),
            pltpu.SemaphoreType.DMA((5,)),
        ]
        + [pltpu.VMEM(x.shape, x.dtype) for x in (charges, basis, transfer, coupling, coords)],
        compiler_params=pltpu.CompilerParams(
            collective_id=0, has_side_effects=True, vmem_limit_bytes=62 * 2**20
        ),
        name="tree",
    )(far_used, charges, coords, basis, transfer, coupling)


def local(charges, coords, basis, near_offsets, near_count, transfer, coupling, far_used):
    coef, before, after, coords_before, coords_after = far_field(
        charges, coords, basis, transfer, coupling, far_used, near_count.shape[0]
    )
    return near_field(
        charges, before, after, coords, coords_before, coords_after, near_offsets, near_count, basis, coef
    )


def solution(mesh):
    in_specs = (
        P(None, ("groups", "leaf", "sub")),
        P(None, ("groups", "leaf", "sub")),
        P(None, ("groups", "leaf", "sub")),
        P(None, ("groups", "leaf", "sub")),
        P(("groups", "leaf", "sub")),
        P(),
        P(),
        P(None, "groups"),
    )
    out_specs = P(None, ("groups", "leaf", "sub"))
    return jax.shard_map(local, mesh=mesh, in_specs=in_specs, out_specs=out_specs, check_vma=False)
```
